128 devices in a mesh: aux: 4 (over y), occ: 32 (over z, x, core).
Axes of the slice: x: 4, y: 4, z: 4, core: 2. Of those that a mesh axis runs over, the one named last changes fastest.
Arguments:
- slab: bfloat16 [128, 8192, 512], P(None, ('aux', 'occ')), may hold values from -6 to 6
- domain_class: int32 [128], replicated, may hold values from 0 to 3
- pairs: int32 [512, 2], P('occ'), may hold values from 0 to 127, as said below
Outputs:
- exchange_ints: bfloat16 [512, 512, 512], P('occ', 'aux')
The draws below stay inside these ranges and needn't reach their ends.
Inputs may be any that keep to these rules, and one draw needn't show every extreme that they name: `pairs`: pair row p belongs to occ index o = p // 16; its first orbital lies in [o * 4, (o + 1) * 4) and its second in [o * 4, min((o + 2) * 4, 128)).
All inputs are finite; a program needn't handle non-finite values.
Results may differ from the reference program's by a relative error of at most 0.0012.
Values may be sent and summed in bfloat16 or wider, within the bound.
A program may use at most 128 MiB of HBM per device.

```python
import jax
import jax.numpy as jnp
from jax import lax

DOM = 512
SLAB = 8192
OCC_DEV = 4
PAIRS_DEV = 16
NOCC = 128
NPAIRS = 512
N_OCC = 32


def draw_pairs(key, part):
    key = jax.random.fold_in(key, 7)
    first_key, second_key = jax.random.split(key)
    rows = jnp.arange(NPAIRS, dtype=jnp.int32)
    owner = rows // PAIRS_DEV
    start = owner * OCC_DEV
    span = jnp.where(owner == N_OCC - 1, OCC_DEV, 2 * OCC_DEV).astype(jnp.int32)
    first = start + jax.random.randint(first_key, (NPAIRS,), 0, OCC_DEV, dtype=jnp.int32)
    second = start + jax.random.randint(second_key, (NPAIRS,), 0, 2 * OCC_DEV, dtype=jnp.int32) % span
    leading = rows % PAIRS_DEV == 0
    first = jnp.where(leading, start, first)
    second = jnp.where(leading, start + span - 1, second)
    return jnp.stack([first, second], axis=1).astype(jnp.int32)


def set_ends(values, stream_key, least, top_value):
    extent = values.shape
    spot = [jax.random.randint(jax.random.fold_in(stream_key, axis), (), 0, extent[axis]) for axis in range(len(extent))]
    values = values.at[tuple(spot)].set(least)
    longest = extent.index(max(extent))
    spot[longest] = (spot[longest] + 1) % extent[longest]
    return values.at[tuple(spot)].set(top_value)


def block_scale(own_key, dims, cuts, least, high):
    def one(dim, blocks):
        heights = jax.random.uniform(jax.random.fold_in(jax.random.fold_in(own_key, 6), dim), (blocks,), jnp.float32, least / len(cuts), high / len(cuts))
        return jnp.repeat(jnp.exp(heights), dims[dim] // blocks).reshape((-1,) + (1,) * (len(dims) - dim - 1))

    factor_of = one(*cuts[0])
    for cut in cuts[1:]:
        factor_of = factor_of * one(*cut)
    return factor_of


def noise(rng, shape, scale, limit, pieces=(), held_as=jnp.bfloat16):
    level = block_scale(rng, shape, pieces, -0.22, 0.18) if pieces else 1.0
    array = jax.random.normal(rng, shape, jnp.float32) * scale * level
    return jnp.minimum(jnp.maximum(array, -limit), limit).astype(held_as)


def setup_inputs(seed: int = 0) -> dict:
    key_of = jax.random.split(jax.random.key(seed), 4)
    slab = noise(key_of[0], (NOCC, SLAB, DOM), 1.0, 6.0, ((1, 128),))
    domain_class = set_ends(jax.random.randint(key_of[1], (NOCC,), 0, 4), jax.random.fold_in(key_of[1], 1), 0, 3).astype(jnp.int32)
    pairs = draw_pairs(jax.random.fold_in(key_of[3], 71), 0)
    return {"slab": slab, "domain_class": domain_class, "pairs": pairs}


def reference(slab, domain_class, pairs):
    size = (domain_class + 1) * (DOM // 4)
    mask = jnp.arange(DOM, dtype=jnp.int32)[None, :] < size[:, None]
    masked = jnp.where(mask[:, None, :], slab, jnp.zeros_like(slab))
    factor = 1.0 / jnp.sqrt(jnp.float32(SLAB))

    def one_pair(pair):
        left = masked[pair[0]]
        right = masked[pair[1]]
        total = lax.dot_general(left, right, (((0,), (0,)), ((), ())), preferred_element_type=jnp.float32)
        return (total * factor).astype(jnp.bfloat16)
    return lax.map(one_pair, pairs)
```

```python
import functools

import jax
import jax.numpy as jnp
from jax import lax
from jax.experimental import pallas as pl
from jax.experimental.pallas import tpu as pltpu
from jax.sharding import PartitionSpec as P

DOM = 512
SLAB = 8192
OCC_DEV = 4
PAIRS_DEV = 16
N_AUX = 4
SIDE = 4
CHIPS = SIDE * SIDE
N_OCC = 2 * CHIPS
ROWS = 64
KLOC = N_OCC * ROWS
HALF = KLOC // 2
COL = DOM // 4
GROUP = 4
NOCC = N_OCC * OCC_DEV
MESH = pl.DeviceIdType.MESH
LEVELS = 32767.0
TINY = 1e-33
BF16 = jnp.bfloat16


def kernel(classes, pairs, slab, out, *scratch):
    cols = scratch[:4]
    (left, total, outbox, inbox, outscale, inscale,
     got, sent, own_sem, mid_got, mid_sent, part_got, part_sent, scale_got, scale_sent) = scratch[4:]
    a = lax.axis_index("aux")
    o = lax.axis_index("occ")
    chip = o // 2
    core = lax.rem(o, 2)
    z, x = chip // SIDE, lax.rem(chip, SIDE)
    start = o * OCC_DEV
    sibling = o + 1 - 2 * core
    mine = pl.ds(core * HALF + chip * ROWS, ROWS)

    barrier = pltpu.get_barrier_semaphore()

    def greet_occ(s, carry):
        pl.semaphore_signal(barrier, inc=1, device_id=(a, lax.rem(o + s, N_OCC)), device_id_type=MESH)
        return carry

    def greet_aux(s, carry):
        pl.semaphore_signal(barrier, inc=1, device_id=(lax.rem(a + s, N_AUX), o), device_id_type=MESH)
        return carry

    lax.fori_loop(1, N_OCC, greet_occ, 0)
    lax.fori_loop(1, N_AUX, greet_aux, 0)

    def column(q):
        return pl.ds(pl.multiple_of(lax.rem(a + q + 1, 4) * COL, COL), COL)

    def own_copy(q, orbital, count, slot):
        return pltpu.make_async_copy(
            slab.at[pl.ds(orbital, count), :, column(q)], cols[q].at[pl.ds(slot, count), mine, :], own_sem.at[q]
        )

    def slab_copy(q, to_chip, to_core, orbital, count, slot):
        return pltpu.make_async_remote_copy(
            src_ref=slab.at[pl.ds(orbital, count), :, column(q)],
            dst_ref=cols[q].at[pl.ds(slot, count), mine, :],
            send_sem=sent.at[q],
            recv_sem=got.at[q],
            device_id=(a, 2 * to_chip + to_core),
            device_id_type=MESH,
        )

    for q in range(4):
        own_copy(q, start, OCC_DEV, 0).start()

        @pl.when(core == 0)
        def _():
            own_copy(q, start + OCC_DEV, OCC_DEV, OCC_DEV).start()

    pl.semaphore_wait(barrier, N_OCC - 1 + N_AUX - 1)

    def send_columns(q):
        ahead = lax.rem(8 * chip + 8, NOCC)

        @pl.when(core == 0)
        def _():
            slab_copy(q, chip, 1, ahead, 4, 4).start()

        @pl.when(core == 1)
        def _():
            slab_copy(q, chip, 0, 8 * chip, 4, 0).start()
            own_copy(q, ahead, 4, 4).start()

        def body(s, carry):
            step = lax.rem(7 * s, CHIPS)
            step = step + core * (CHIPS - 2 * step)
            to = lax.rem(z + step // SIDE, SIDE) * SIDE + lax.rem(x + lax.rem(step, SIDE), SIDE)
            base = 8 * to
            beyond = lax.rem(base + 8, NOCC)

            @pl.when(core == 0)
            def _():
                slab_copy(q, to, 0, base, 8, 0).start()
                slab_copy(q, to, 1, beyond, 4, 4).start()

            @pl.when(core == 1)
            def _():
                slab_copy(q, to, 0, base, 4, 0).start()
                slab_copy(q, to, 1, base + 4, 4, 0).start()
                slab_copy(q, to, 1, beyond, 4, 4).start()

            return carry

        lax.fori_loop(1, CHIPS, body, 0)

    for q in range(4):
        send_columns(q)

    def wait_bytes(ref, sem):
        pltpu.make_async_copy(ref, ref, sem).wait()

    def remote_part(q):
        return cols[q].at[:, pl.ds(0, 23 * ROWS), :]

    def middle_copy(q):
        half = pl.ds(core * HALF, HALF)
        return pltpu.make_async_remote_copy(
            src_ref=cols[q].at[pl.ds(4 - 4 * core, 4), half, :],
            dst_ref=cols[q].at[pl.ds(4 * core, 4), half, :],
            send_sem=mid_sent.at[q],
            recv_sem=mid_got.at[q],
            device_id=(a, sibling),
            device_id_type=MESH,
        )

    def arrive(q):
        wait_bytes(cols[q].at[:, pl.ds(0, ROWS), :], own_sem.at[q])
        wait_bytes(remote_part(q), got.at[q])
        middle_copy(q).start()

    def settle(q):
        middle_copy(q).wait()
        for i in range(OCC_DEV):
            left[i, q * COL:(q + 1) * COL, :] = cols[q][i].T

    factor = 1.0 / jnp.sqrt(jnp.float32(SLAB))

    def weight(p, m, n):
        keep_m = lax.rem(a + m + 1, 4) <= classes[pairs[p, 0]]
        keep_n = lax.rem(a + n + 1, 4) <= classes[pairs[p, 1]]
        return jnp.where(jnp.logical_and(keep_m, keep_n), factor, 0.0)

    def emit(p, m, n, block):
        block = block * weight(p, m, n)
        if m == 3:
            total[n, p] = block
        else:
            top = jnp.maximum(jnp.max(jnp.abs(block), axis=0, keepdims=True), TINY)
            outscale[m, n, pl.ds(p, 1), :] = top * (1.0 / LEVELS)
            outbox[m, n, p] = jnp.round(block * (LEVELS / top)).astype(jnp.int32).astype(jnp.int16)

    def part_copy(m, n, g):
        some = pl.ds(g * GROUP, GROUP)
        return pltpu.make_async_remote_copy(
            src_ref=outbox.at[m, n, some],
            dst_ref=inbox.at[m, n, some],
            send_sem=part_sent.at[m, n],
            recv_sem=part_got.at[m, n],
            device_id=(lax.rem(a + m + 1, 4), o),
            device_id_type=MESH,
        )

    def scale_copy(m, n):
        return pltpu.make_async_remote_copy(
            src_ref=outscale.at[m, n],
            dst_ref=inscale.at[m, n],
            send_sem=scale_sent.at[m, n],
            recv_sem=scale_got.at[m, n],
            device_id=(lax.rem(a + m + 1, 4), o),
            device_id_type=MESH,
        )

    def multiply(ms, ns):
        lo, hi = ms[0], ms[-1] + 1

        def group(g, carry):
            def one(t, carry):
                p = g * GROUP + t
                i = jnp.clip(pairs[p, 0] - start, 0, OCC_DEV - 1)
                j = jnp.clip(pairs[p, 1] - start, 0, 2 * OCC_DEV - 1)
                rows = left[i, lo * COL:hi * COL, :]
                for n in ns:
                    block = jnp.dot(rows, cols[n][j], preferred_element_type=jnp.float32)
                    for m in ms:
                        emit(p, m, n, block[(m - lo) * COL:(m - lo + 1) * COL])
                return carry

            lax.fori_loop(0, GROUP, one, 0)
            for m in ms:
                if m < 3:
                    for n in ns:
                        part_copy(m, n, g).start()
            return carry

        lax.fori_loop(0, PAIRS_DEV // GROUP, group, 0)
        for m in ms:
            if m < 3:
                for n in ns:
                    scale_copy(m, n).start()

    for q in range(4):
        arrive(q)
        settle(q)
        multiply(list(range(min(q + 1, 3))), [q])
        if 0 < q < 3:
            multiply([q], list(range(q)))
    multiply([3], [0, 1, 2, 3])

    for n in range(4):
        for m in range(3):
            wait_bytes(inbox.at[m, n], part_got.at[m, n])
            wait_bytes(inscale.at[m, n], scale_got.at[m, n])

    def finish(p, carry):
        for n in range(4):
            value = total[n, p]
            for m in range(3):
                there = (n + m + 1) % 4
                part = inbox[m, there, p].astype(jnp.int32).astype(jnp.float32)
                value = value + part * inscale[m, there, pl.ds(p, 1), :]
            out[p, :, column(n)] = value.astype(BF16)
        return carry

    lax.fori_loop(0, PAIRS_DEV, finish, 0)

    for q in range(4):
        wait_bytes(remote_part(q), sent.at[q])
    for n in range(4):
        for m in range(3):
            wait_bytes(outbox.at[m, n], part_sent.at[m, n])
            wait_bytes(outscale.at[m, n], scale_sent.at[m, n])


def on_device(slab, domain_class, pairs):
    dma = pltpu.SemaphoreType.DMA
    return pl.pallas_call(
        kernel,
        out_shape=jax.ShapeDtypeStruct((PAIRS_DEV, COL, DOM), BF16),
        in_specs=[
            pl.BlockSpec(memory_space=pltpu.SMEM),
            pl.BlockSpec(memory_space=pltpu.SMEM),
            pl.BlockSpec(memory_space=pl.ANY),
        ],
        out_specs=pl.BlockSpec(memory_space=pltpu.VMEM),
        scratch_shapes=[pltpu.VMEM((2 * OCC_DEV, KLOC, COL), BF16)] * 4 + [
            pltpu.VMEM((OCC_DEV, DOM, KLOC), BF16),
            pltpu.VMEM((4, PAIRS_DEV, COL, COL), jnp.float32),
            pltpu.VMEM((3, 4, PAIRS_DEV, COL, COL), jnp.int16),
            pltpu.VMEM((3, 4, PAIRS_DEV, COL, COL), jnp.int16),
            pltpu.VMEM((3, 4, PAIRS_DEV, COL), jnp.float32),
            pltpu.VMEM((3, 4, PAIRS_DEV, COL), jnp.float32),
            dma((4,)), dma((4,)), dma((4,)), dma((4,)), dma((4,)),
            dma((3, 4)), dma((3, 4)), dma((3, 4)), dma((3, 4)),
        ],
        compiler_params=pltpu.CompilerParams(
            collective_id=0, has_side_effects=True, vmem_limit_bytes=56 << 20
        ),
        cost_estimate=pl.CostEstimate(flops=17_000_000_000, bytes_accessed=12 << 20, transcendentals=0),
    )(domain_class, pairs, slab)


def solution(mesh):
    in_specs = (P(None, ("aux", "occ"), None), P(), P("occ", None))
    out_specs = P("occ", "aux", None)
    return jax.shard_map(
        on_device, mesh=mesh, in_specs=in_specs, out_specs=out_specs, check_vma=False
    )
```

```python
import functools

import jax
import jax.numpy as jnp
from jax import lax
from jax.experimental import pallas as pl
from jax.experimental.pallas import tpu as pltpu
from jax.sharding import PartitionSpec as P

DOM = 512
SLAB = 8192
OCC_DEV = 4
PAIRS_DEV = 16
N_AUX = 4
SIDE = 4
CHIPS = SIDE * SIDE
N_OCC = 2 * CHIPS
ROWS = 64
KLOC = N_OCC * ROWS
HALF = KLOC // 2
COL = DOM // 4
GROUP = 4
NOCC = N_OCC * OCC_DEV
MESH = pl.DeviceIdType.MESH
LEVELS = 32767.0
TINY = 1e-33
BF16 = jnp.bfloat16
EVENTS = tuple((part, q) for q in range(4) for part in "BAC")
WINDOW = 5


def kernel(classes, pairs, slab, out, *scratch):
    cols = scratch[:4]
    (left, total, outbox, inbox, outscale, inscale,
     got, sent, kept, mid_got, mid_sent, part_got, part_sent, scale_got, scale_sent) = scratch[4:]
    a = lax.axis_index("aux")
    o = lax.axis_index("occ")
    chip = o // 2
    core = lax.rem(o, 2)
    z, x = chip // SIDE, lax.rem(chip, SIDE)
    start = o * OCC_DEV
    sibling = o + 1 - 2 * core
    mine = pl.ds(core * HALF + chip * ROWS, ROWS)

    barrier = pltpu.get_barrier_semaphore()

    def greet_occ(s, carry):
        pl.semaphore_signal(barrier, inc=1, device_id=(a, lax.rem(o + s, N_OCC)), device_id_type=MESH)
        return carry

    def greet_aux(s, carry):
        pl.semaphore_signal(barrier, inc=1, device_id=(lax.rem(a + s, N_AUX), o), device_id_type=MESH)
        return carry

    lax.fori_loop(1, N_OCC, greet_occ, 0)
    lax.fori_loop(1, N_AUX, greet_aux, 0)

    def column(q):
        return pl.ds(pl.multiple_of(lax.rem(a + q + 1, 4) * COL, COL), COL)

    def place(part, to_chip):
        if part == "A":
            return 8 * to_chip, 0, 0
        if part == "B":
            return 8 * to_chip + 4, core, 4 - 4 * core
        return lax.rem(8 * to_chip + 8, NOCC), 1, 4

    def keep_copy(part, q):
        orbital, _, slot = place(part, chip)
        e = EVENTS.index((part, q))
        return pltpu.make_async_copy(
            slab.at[pl.ds(orbital, 4), :, column(q)], cols[q].at[pl.ds(slot, 4), mine, :], kept.at[e]
        )

    def slab_copy(part, q, to_chip):
        orbital, to_core, slot = place(part, to_chip)
        e = EVENTS.index((part, q))
        return pltpu.make_async_remote_copy(
            src_ref=slab.at[pl.ds(orbital, 4), :, column(q)],
            dst_ref=cols[q].at[pl.ds(slot, 4), mine, :],
            send_sem=sent.at[e],
            recv_sem=got.at[e],
            device_id=(a, 2 * to_chip + to_core),
            device_id_type=MESH,
        )

    for part, q in EVENTS:
        if part == "B":
            keep_copy(part, q).start()
        else:
            @pl.when(core == (part == "C"))
            def _():
                keep_copy(part, q).start()

    pl.semaphore_wait(barrier, N_OCC - 1 + N_AUX - 1)

    def send(part, q):
        if part != "B":
            @pl.when(core == (part == "A"))
            def _():
                slab_copy(part, q, chip).start()

        def body(s, carry):
            step = lax.rem(7 * s, CHIPS)
            step = step + core * (CHIPS - 2 * step)
            to = lax.rem(z + step // SIDE, SIDE) * SIDE + lax.rem(x + lax.rem(step, SIDE), SIDE)
            slab_copy(part, q, to).start()
            return carry

        lax.fori_loop(1, CHIPS, body, 0)

    for part, q in EVENTS[:WINDOW]:
        send(part, q)

    def wait_bytes(ref, sem):
        pltpu.make_async_copy(ref, ref, sem).wait()

    def orbitals(q, sources):
        return cols[q].at[pl.ds(0, 4), pl.ds(0, sources * ROWS), :]

    def middle_copy(q):
        half = pl.ds(core * HALF, HALF)
        return pltpu.make_async_remote_copy(
            src_ref=cols[q].at[pl.ds(4 - 4 * core, 4), half, :],
            dst_ref=cols[q].at[pl.ds(4 * core, 4), half, :],
            send_sem=mid_sent.at[q],
            recv_sem=mid_got.at[q],
            device_id=(a, sibling),
            device_id_type=MESH,
        )

    def settle(q):
        for i in range(OCC_DEV):
            left[i, q * COL:(q + 1) * COL, :] = cols[q][i].T

    def take(part, q):
        e = EVENTS.index((part, q))
        if part == "B":
            wait_bytes(orbitals(q, 1), kept.at[e])
            wait_bytes(orbitals(q, CHIPS - 1), got.at[e])
            middle_copy(q).start()
            middle_copy(q).wait()

            @pl.when(core == 1)
            def _():
                settle(q)
        else:
            @pl.when(core == (part == "C"))
            def _():
                wait_bytes(orbitals(q, 1), kept.at[e])
                wait_bytes(orbitals(q, N_OCC - 1), got.at[e])
                if part == "A":
                    settle(q)

    factor = 1.0 / jnp.sqrt(jnp.float32(SLAB))

    def weight(p, m, n):
        keep_m = lax.rem(a + m + 1, 4) <= classes[pairs[p, 0]]
        keep_n = lax.rem(a + n + 1, 4) <= classes[pairs[p, 1]]
        return jnp.where(jnp.logical_and(keep_m, keep_n), factor, 0.0)

    def emit(p, m, n, block):
        block = block * weight(p, m, n)
        if m == 3:
            total[n, p] = block
        else:
            top = jnp.maximum(jnp.max(jnp.abs(block), axis=0, keepdims=True), TINY)
            outscale[m, n, pl.ds(p, 1), :] = top * (1.0 / LEVELS)
            outbox[m, n, p] = jnp.round(block * (LEVELS / top)).astype(jnp.int32).astype(jnp.int16)

    def part_copy(m, n, g):
        some = pl.ds(g * GROUP, GROUP)
        return pltpu.make_async_remote_copy(
            src_ref=outbox.at[m, n, some],
            dst_ref=inbox.at[m, n, some],
            send_sem=part_sent.at[m, n],
            recv_sem=part_got.at[m, n],
            device_id=(lax.rem(a + m + 1, 4), o),
            device_id_type=MESH,
        )

    def scale_copy(m, n):
        return pltpu.make_async_remote_copy(
            src_ref=outscale.at[m, n],
            dst_ref=inscale.at[m, n],
            send_sem=scale_sent.at[m, n],
            recv_sem=scale_got.at[m, n],
            device_id=(lax.rem(a + m + 1, 4), o),
            device_id_type=MESH,
        )

    def multiply(ms, ns):
        lo, hi = ms[0], ms[-1] + 1

        def group(g, carry):
            def one(t, carry):
                p = g * GROUP + t
                i = jnp.clip(pairs[p, 0] - start, 0, OCC_DEV - 1)
                j = jnp.clip(pairs[p, 1] - start, 0, 2 * OCC_DEV - 1)
                rows = left[i, lo * COL:hi * COL, :]
                for n in ns:
                    block = jnp.dot(rows, cols[n][j], preferred_element_type=jnp.float32)
                    for m in ms:
                        emit(p, m, n, block[(m - lo) * COL:(m - lo + 1) * COL])
                return carry

            lax.fori_loop(0, GROUP, one, 0)
            for m in ms:
                if m < 3:
                    for n in ns:
                        part_copy(m, n, g).start()
            return carry

        lax.fori_loop(0, PAIRS_DEV // GROUP, group, 0)
        for m in ms:
            if m < 3:
                for n in ns:
                    scale_copy(m, n).start()

    here = []
    lefts, rights = [[], []], [[], []]
    for e, (part, q) in enumerate(EVENTS):
        take(part, q)
        if e + WINDOW < len(EVENTS):
            send(*EVENTS[e + WINDOW])
        here.append((part, q))
        for who in range(2):
            needs = "AB" if who == 0 else "BC"
            old_left, old_right = lefts[who], rights[who]
            new_left = [q] if part == needs[0] else []
            new_right = [n for n in range(4) if n not in old_right and all((h, n) in here for h in needs)]
            lefts[who], rights[who] = old_left + new_left, old_right + new_right
            remote = [m for m in lefts[who] if m < 3]

            @pl.when(core == who)
            def _():
                if new_right and remote:
                    multiply(remote, new_right)
                if new_left and q < 3 and old_right:
                    multiply(new_left, old_right)
                if 3 in old_left and new_right:
                    multiply([3], new_right)
                if 3 in new_left and rights[who]:
                    multiply([3], rights[who])

    for n in range(4):
        for m in range(3):
            wait_bytes(inbox.at[m, n], part_got.at[m, n])
            wait_bytes(inscale.at[m, n], scale_got.at[m, n])

    def finish(p, carry):
        for n in range(4):
            value = total[n, p]
            for m in range(3):
                there = (n + m + 1) % 4
                part = inbox[m, there, p].astype(jnp.int32).astype(jnp.float32)
                value = value + part * inscale[m, there, pl.ds(p, 1), :]
            out[p, :, column(n)] = value.astype(BF16)
        return carry

    lax.fori_loop(0, PAIRS_DEV, finish, 0)

    for e, (part, q) in enumerate(EVENTS):
        wait_bytes(orbitals(q, CHIPS - 1), sent.at[e])
        if part != "B":
            @pl.when(core == (part == "A"))
            def _():
                wait_bytes(orbitals(q, 1), sent.at[e])

    for n in range(4):
        for m in range(3):
            wait_bytes(outbox.at[m, n], part_sent.at[m, n])
            wait_bytes(outscale.at[m, n], scale_sent.at[m, n])


def on_device(slab, domain_class, pairs):
    dma = pltpu.SemaphoreType.DMA
    return pl.pallas_call(
        kernel,
        out_shape=jax.ShapeDtypeStruct((PAIRS_DEV, COL, DOM), BF16),
        in_specs=[
            pl.BlockSpec(memory_space=pltpu.SMEM),
            pl.BlockSpec(memory_space=pltpu.SMEM),
            pl.BlockSpec(memory_space=pl.ANY),
        ],
        out_specs=pl.BlockSpec(memory_space=pltpu.VMEM),
        scratch_shapes=[pltpu.VMEM((2 * OCC_DEV, KLOC, COL), BF16)] * 4 + [
            pltpu.VMEM((OCC_DEV, DOM, KLOC), BF16),
            pltpu.VMEM((4, PAIRS_DEV, COL, COL), jnp.float32),
            pltpu.VMEM((3, 4, PAIRS_DEV, COL, COL), jnp.int16),
            pltpu.VMEM((3, 4, PAIRS_DEV, COL, COL), jnp.int16),
            pltpu.VMEM((3, 4, PAIRS_DEV, COL), jnp.float32),
            pltpu.VMEM((3, 4, PAIRS_DEV, COL), jnp.float32),
            dma((12,)), dma((12,)), dma((12,)), dma((4,)), dma((4,)),
            dma((3, 4)), dma((3, 4)), dma((3, 4)), dma((3, 4)),
        ],
        compiler_params=pltpu.CompilerParams(
            collective_id=0, has_side_effects=True, vmem_limit_bytes=56 << 20
        ),
        cost_estimate=pl.CostEstimate(flops=17_000_000_000, bytes_accessed=12 << 20, transcendentals=0),
    )(domain_class, pairs, slab)


def solution(mesh):
    in_specs = (P(None, ("aux", "occ"), None), P(), P("occ", None))
    out_specs = P("occ", "aux", None)
    return jax.shard_map(
        on_device, mesh=mesh, in_specs=in_specs, out_specs=out_specs, check_vma=False
    )
```

```python
import functools

import jax
import jax.numpy as jnp
from jax import lax
from jax.experimental import pallas as pl
from jax.experimental.pallas import tpu as pltpu
from jax.sharding import PartitionSpec as P

DOM = 512
SLAB = 8192
OCC_DEV = 4
PAIRS_DEV = 16
N_AUX = 4
SIDE = 4
CHIPS = SIDE * SIDE
N_OCC = 2 * CHIPS
ROWS = 64
KLOC = N_OCC * ROWS
HALF = KLOC // 2
COL = DOM // 4
GROUP = 4
UNROLL = 4
NOCC = N_OCC * OCC_DEV
MESH = pl.DeviceIdType.MESH
LEVELS = 32767.0
TINY = 1e-33
BF16 = jnp.bfloat16
EVENTS = tuple((part, q) for part in "ABC" for q in range(4))
HELD = PAIRS_DEV // 2


def kernel(classes, pairs, slab, out, *scratch):
    cols = scratch[:4]
    (left, total, hold, outbox, inbox, outscale, inscale,
     got, sent, kept, mid_got, mid_sent, part_got, part_sent, scale_got, scale_sent) = scratch[4:]
    a = lax.axis_index("aux")
    o = lax.axis_index("occ")
    chip = o // 2
    core = lax.rem(o, 2)
    z, x = chip // SIDE, lax.rem(chip, SIDE)
    start = o * OCC_DEV
    sibling = o + 1 - 2 * core
    mine = pl.ds(core * HALF + chip * ROWS, ROWS)

    barrier = pltpu.get_barrier_semaphore()

    def greet_occ(s, carry):
        pl.semaphore_signal(barrier, inc=1, device_id=(a, lax.rem(o + s, N_OCC)), device_id_type=MESH)
        return carry

    def greet_aux(s, carry):
        pl.semaphore_signal(barrier, inc=1, device_id=(lax.rem(a + s, N_AUX), o), device_id_type=MESH)
        return carry

    lax.fori_loop(1, N_OCC, greet_occ, 0)
    greet_aux(1, 0)
    greet_aux(N_AUX - 1, 0)

    def column(q):
        return pl.ds(q * COL, COL)

    def place(part, to_chip):
        if part == "A":
            return 8 * to_chip, 0, 0
        if part == "B":
            return 8 * to_chip + 4, core, 4 - 4 * core
        return lax.rem(8 * to_chip + 8, NOCC), 1, 4

    def keep_copy(part, q):
        orbital, _, slot = place(part, chip)
        e = EVENTS.index((part, q))
        return pltpu.make_async_copy(
            slab.at[pl.ds(orbital, 4), :, column(q)], cols[q].at[pl.ds(slot, 4), mine, :], kept.at[e]
        )

    def slab_copy(part, q, to_chip):
        orbital, to_core, slot = place(part, to_chip)
        e = EVENTS.index((part, q))
        return pltpu.make_async_remote_copy(
            src_ref=slab.at[pl.ds(orbital, 4), :, column(q)],
            dst_ref=cols[q].at[pl.ds(slot, 4), mine, :],
            send_sem=sent.at[e],
            recv_sem=got.at[e],
            device_id=(a, 2 * to_chip + to_core),
            device_id_type=MESH,
        )

    for part, q in EVENTS:
        if part == "B":
            keep_copy(part, q).start()
        else:
            @pl.when(core == (part == "C"))
            def _():
                keep_copy(part, q).start()

    pl.semaphore_wait(barrier, N_OCC + 1)

    def send(part, q):
        if part != "B":
            @pl.when(core == (part == "A"))
            def _():
                slab_copy(part, q, chip).start()

        def body(s, carry):
            step = lax.rem(7 * s, CHIPS)
            step = step + core * (CHIPS - 2 * step)
            to = lax.rem(z + step // SIDE, SIDE) * SIDE + lax.rem(x + lax.rem(step, SIDE), SIDE)
            slab_copy(part, q, to).start()
            return carry

        lax.fori_loop(1, CHIPS, body, 0)

    for part, q in EVENTS:
        send(part, q)

    def wait_bytes(ref, sem):
        pltpu.make_async_copy(ref, ref, sem).wait()

    def orbitals(q, sources):
        return cols[q].at[pl.ds(0, 4), pl.ds(0, sources * ROWS), :]

    def middle_copy(q):
        half = pl.ds(core * HALF, HALF)
        return pltpu.make_async_remote_copy(
            src_ref=cols[q].at[pl.ds(4 - 4 * core, 4), half, :],
            dst_ref=cols[q].at[pl.ds(4 * core, 4), half, :],
            send_sem=mid_sent.at[q],
            recv_sem=mid_got.at[q],
            device_id=(a, sibling),
            device_id_type=MESH,
        )

    def arrived(part, q, sources):
        e = EVENTS.index((part, q))
        wait_bytes(orbitals(q, 1), kept.at[e])
        wait_bytes(orbitals(q, sources), got.at[e])

    def settle(q):
        slot = pl.multiple_of(lax.rem(q + 7 - a, 4) * COL, COL)
        for i in range(OCC_DEV):
            left[i, pl.ds(slot, COL), :] = cols[q][i].T

    factor = 1.0 / jnp.sqrt(jnp.float32(SLAB))

    def weight(p, m, n):
        keep_m = lax.rem(a + m + 1, 4) <= classes[pairs[p, 0]]
        keep_n = n <= classes[pairs[p, 1]]
        return jnp.where(jnp.logical_and(keep_m, keep_n), factor, 0.0)

    def pack(p, m, n, block):
        top = jnp.maximum(jnp.max(jnp.abs(block), axis=0, keepdims=True), TINY)
        outscale[m, n, pl.ds(p, 1), :] = top * (1.0 / LEVELS)
        outbox[m, n, p] = jnp.round(block * (LEVELS / top)).astype(jnp.int32).astype(jnp.int16)

    def unpack(p, m, n):
        return inbox[m, n, p].astype(jnp.int32).astype(jnp.float32) * inscale[m, n, pl.ds(p, 1), :]

    def toward(m, h):
        up = m == 0 or (m == 1 and h == 0)
        return lax.rem(a + (1 if up else N_AUX - 1), N_AUX), o

    def part_copy(m, n, h, g):
        some = pl.ds(g * GROUP, GROUP)
        return pltpu.make_async_remote_copy(
            src_ref=outbox.at[m, n, some],
            dst_ref=inbox.at[m, n, some],
            send_sem=part_sent.at[m, n, h],
            recv_sem=part_got.at[m, n, h],
            device_id=toward(m, h),
            device_id_type=MESH,
        )

    def half(ref, m, n, h):
        return ref.at[m, n, pl.ds(h * HELD, HELD)]

    def scale_copy(m, n, h):
        return pltpu.make_async_remote_copy(
            src_ref=half(outscale, m, n, h),
            dst_ref=half(inscale, m, n, h),
            send_sem=scale_sent.at[m, n, h],
            recv_sem=scale_got.at[m, n, h],
            device_id=toward(m, h),
            device_id_type=MESH,
        )

    def multiply(n, h):
        direct, held = (2, 0) if h == 0 else (0, 2)

        def group(g, carry):
            def one(t, carry):
                p = g * GROUP + t
                i = jnp.clip(pairs[p, 0] - start, 0, OCC_DEV - 1)
                j = jnp.clip(pairs[p, 1] - start, 0, 2 * OCC_DEV - 1)
                block = jnp.dot(left[i], cols[n][j], preferred_element_type=jnp.float32)
                for m in range(4):
                    part = block[m * COL:(m + 1) * COL] * weight(p, m, n)
                    if m == 3:
                        total[n, p] = part
                    elif m == held:
                        hold[h, n, p - h * HELD] = part
                    else:
                        pack(p, m, n, part)
                return carry

            lax.fori_loop(0, GROUP, one, 0, unroll=UNROLL)
            part_copy(1, n, h, g).start()
            part_copy(direct, n, h, g).start()
            return carry

        lax.fori_loop(h * (HELD // GROUP), (h + 1) * (HELD // GROUP), group, 0)
        scale_copy(1, n, h).start()
        scale_copy(direct, n, h).start()

    def relay(n, h):
        m = 0 if h == 0 else 2
        wait_bytes(half(inbox, 1, n, h), part_got.at[1, n, h])
        wait_bytes(half(inscale, 1, n, h), scale_got.at[1, n, h])

        def group(g, carry):
            def one(t, carry):
                p = g * GROUP + t
                pack(p, m, n, hold[h, n, p - h * HELD] + unpack(p, 1, n))
                return carry

            lax.fori_loop(0, GROUP, one, 0, unroll=UNROLL)
            part_copy(m, n, h, g).start()
            return carry

        lax.fori_loop(h * (HELD // GROUP), (h + 1) * (HELD // GROUP), group, 0)
        scale_copy(m, n, h).start()

    def finish(n, h):
        for m in (0, 2):
            wait_bytes(half(inbox, m, n, h), part_got.at[m, n, h])
            wait_bytes(half(inscale, m, n, h), scale_got.at[m, n, h])

        def one(p, carry):
            out[p, :, column(n)] = (total[n, p] + unpack(p, 0, n) + unpack(p, 2, n)).astype(BF16)
            return carry

        lax.fori_loop(h * HELD, (h + 1) * HELD, one, 0)

    @pl.when(core == 0)
    def _():
        for q in range(4):
            arrived("A", q, N_OCC - 1)
            settle(q)

    @pl.when(core == 1)
    def _():
        for q in range(4):
            arrived("B", q, CHIPS - 1)
            middle_copy(q).start()
        for q in range(4):
            middle_copy(q).wait()
            settle(q)

    for n in range(4):
        @pl.when(core == 0)
        def _():
            arrived("B", n, CHIPS - 1)
            middle_copy(n).start()
            middle_copy(n).wait()

        @pl.when(core == 1)
        def _():
            arrived("C", n, N_OCC - 1)

        multiply(n, 0)
        if n > 0:
            relay(n - 1, 0)
            relay(n - 1, 1)
        multiply(n, 1)

    relay(3, 0)
    relay(3, 1)
    for n in range(4):
        for h in range(2):
            finish(n, h)

    for e, (part, q) in enumerate(EVENTS):
        wait_bytes(orbitals(q, CHIPS - 1), sent.at[e])
        if part != "B":
            @pl.when(core == (part == "A"))
            def _():
                wait_bytes(orbitals(q, 1), sent.at[e])

    for n in range(4):
        for m in range(3):
            for h in range(2):
                wait_bytes(half(outbox, m, n, h), part_sent.at[m, n, h])
                wait_bytes(half(outscale, m, n, h), scale_sent.at[m, n, h])


def on_device(slab, domain_class, pairs):
    dma = pltpu.SemaphoreType.DMA
    return pl.pallas_call(
        kernel,
        out_shape=jax.ShapeDtypeStruct((PAIRS_DEV, COL, DOM), BF16),
        in_specs=[
            pl.BlockSpec(memory_space=pltpu.SMEM),
            pl.BlockSpec(memory_space=pltpu.SMEM),
            pl.BlockSpec(memory_space=pl.ANY),
        ],
        out_specs=pl.BlockSpec(memory_space=pltpu.VMEM),
        scratch_shapes=[pltpu.VMEM((2 * OCC_DEV, KLOC, COL), BF16)] * 4 + [
            pltpu.VMEM((OCC_DEV, DOM, KLOC), BF16),
            pltpu.VMEM((4, PAIRS_DEV, COL, COL), jnp.float32),
            pltpu.VMEM((2, 4, HELD, COL, COL), jnp.float32),
            pltpu.VMEM((3, 4, PAIRS_DEV, COL, COL), jnp.int16),
            pltpu.VMEM((3, 4, PAIRS_DEV, COL, COL), jnp.int16),
            pltpu.VMEM((3, 4, PAIRS_DEV, COL), jnp.float32),
            pltpu.VMEM((3, 4, PAIRS_DEV, COL), jnp.float32),
            dma((12,)), dma((12,)), dma((12,)), dma((4,)), dma((4,)),
            dma((3, 4, 2)), dma((3, 4, 2)), dma((3, 4, 2)), dma((3, 4, 2)),
        ],
        compiler_params=pltpu.CompilerParams(
            collective_id=0, has_side_effects=True, vmem_limit_bytes=58 << 20
        ),
        cost_estimate=pl.CostEstimate(flops=17_000_000_000, bytes_accessed=12 << 20, transcendentals=0),
    )(domain_class, pairs, slab)


def solution(mesh):
    in_specs = (P(None, ("aux", "occ"), None), P(), P("occ", None))
    out_specs = P("occ", "aux", None)
    return jax.shard_map(
        on_device, mesh=mesh, in_specs=in_specs, out_specs=out_specs, check_vma=False
    )
```

```python
import functools

import jax
import jax.numpy as jnp
from jax import lax
from jax.experimental import pallas as pl
from jax.experimental.pallas import tpu as pltpu
from jax.sharding import PartitionSpec as P

DOM = 512
SLAB = 8192
OCC_DEV = 4
PAIRS_DEV = 16
N_AUX = 4
SIDE = 4
CHIPS = SIDE * SIDE
N_OCC = 2 * CHIPS
ROWS = 64
KLOC = N_OCC * ROWS
HALF = KLOC // 2
COL = DOM // 4
GROUP = 4
UNROLL = 4
NOCC = N_OCC * OCC_DEV
MESH = pl.DeviceIdType.MESH
LEVELS = 32767.0
TINY = 1e-33
BF16 = jnp.bfloat16
EVENTS = tuple((part, q) for part in "ABC" for q in range(4))
HELD = PAIRS_DEV // 2
FARTHEST = sorted(
    [(dz, dx) for dz in range(SIDE) for dx in range(SIDE) if dz or dx],
    key=lambda d: -sum(min(step, SIDE - step) for step in d),
)


def kernel(classes, pairs, slab, out, *scratch):
    cols = scratch[:4]
    (left, total, hold, outbox, inbox, outscale, inscale,
     got, sent, kept, mid_got, mid_sent, part_got, part_sent, scale_got, scale_sent) = scratch[4:]
    a = lax.axis_index("aux")
    o = lax.axis_index("occ")
    chip = o // 2
    core = lax.rem(o, 2)
    z, x = chip // SIDE, lax.rem(chip, SIDE)
    start = o * OCC_DEV
    sibling = o + 1 - 2 * core
    mine = pl.ds(core * HALF + chip * ROWS, ROWS)

    barrier = pltpu.get_barrier_semaphore()

    def greet_occ(s, carry):
        pl.semaphore_signal(barrier, inc=1, device_id=(a, lax.rem(o + s, N_OCC)), device_id_type=MESH)
        return carry

    def greet_aux(s, carry):
        pl.semaphore_signal(barrier, inc=1, device_id=(lax.rem(a + s, N_AUX), o), device_id_type=MESH)
        return carry

    lax.fori_loop(1, N_OCC, greet_occ, 0)
    greet_aux(1, 0)
    greet_aux(N_AUX - 1, 0)

    def column(q):
        return pl.ds(q * COL, COL)

    def place(part, to_chip):
        if part == "A":
            return 8 * to_chip, 0, 0
        if part == "B":
            return 8 * to_chip + 4, core, 4 - 4 * core
        return lax.rem(8 * to_chip + 8, NOCC), 1, 4

    def keep_copy(part, q):
        orbital, _, slot = place(part, chip)
        e = EVENTS.index((part, q))
        return pltpu.make_async_copy(
            slab.at[pl.ds(orbital, 4), :, column(q)], cols[q].at[pl.ds(slot, 4), mine, :], kept.at[e]
        )

    def slab_copy(part, q, to_chip):
        orbital, to_core, slot = place(part, to_chip)
        e = EVENTS.index((part, q))
        return pltpu.make_async_remote_copy(
            src_ref=slab.at[pl.ds(orbital, 4), :, column(q)],
            dst_ref=cols[q].at[pl.ds(slot, 4), mine, :],
            send_sem=sent.at[e],
            recv_sem=got.at[e],
            device_id=(a, 2 * to_chip + to_core),
            device_id_type=MESH,
        )

    for part, q in EVENTS:
        if part == "B":
            keep_copy(part, q).start()
        else:
            @pl.when(core == (part == "C"))
            def _():
                keep_copy(part, q).start()

    pl.semaphore_wait(barrier, N_OCC + 1)

    def send(part, q):
        if part != "B":
            @pl.when(core == (part == "A"))
            def _():
                slab_copy(part, q, chip).start()

        for dz, dx in FARTHEST:
            dz = dz + core * ((SIDE - dz) % SIDE - dz)
            dx = dx + core * ((SIDE - dx) % SIDE - dx)
            to = lax.rem(z + dz, SIDE) * SIDE + lax.rem(x + dx, SIDE)
            slab_copy(part, q, to).start()

    for part, q in EVENTS:
        send(part, q)

    def wait_bytes(ref, sem):
        pltpu.make_async_copy(ref, ref, sem).wait()

    def orbitals(q, sources):
        return cols[q].at[pl.ds(0, 4), pl.ds(0, sources * ROWS), :]

    def middle_copy(q):
        half = pl.ds(core * HALF, HALF)
        return pltpu.make_async_remote_copy(
            src_ref=cols[q].at[pl.ds(4 - 4 * core, 4), half, :],
            dst_ref=cols[q].at[pl.ds(4 * core, 4), half, :],
            send_sem=mid_sent.at[q],
            recv_sem=mid_got.at[q],
            device_id=(a, sibling),
            device_id_type=MESH,
        )

    def arrived(part, q, sources):
        e = EVENTS.index((part, q))
        wait_bytes(orbitals(q, 1), kept.at[e])
        wait_bytes(orbitals(q, sources), got.at[e])

    def settle(q):
        slot = pl.multiple_of(lax.rem(q + 7 - a, 4) * COL, COL)
        for i in range(OCC_DEV):
            left[i, pl.ds(slot, COL), :] = cols[q][i].T

    factor = 1.0 / jnp.sqrt(jnp.float32(SLAB))

    def weight(p, m, n):
        keep_m = lax.rem(a + m + 1, 4) <= classes[pairs[0, p]]
        keep_n = n <= classes[pairs[1, p]]
        return jnp.where(jnp.logical_and(keep_m, keep_n), factor, 0.0)

    def pack(p, m, n, block):
        top = jnp.maximum(jnp.max(jnp.abs(block), axis=0, keepdims=True), TINY)
        outscale[m, n, pl.ds(p, 1), :] = top * (1.0 / LEVELS)
        outbox[m, n, p] = jnp.round(block * (LEVELS / top)).astype(jnp.int32).astype(jnp.int16)

    def unpack(p, m, n):
        return inbox[m, n, p].astype(jnp.int32).astype(jnp.float32) * inscale[m, n, pl.ds(p, 1), :]

    def toward(m, h):
        up = m == 0 or (m == 1 and h == 0)
        return lax.rem(a + (1 if up else N_AUX - 1), N_AUX), o

    def part_copy(m, n, h, g):
        some = pl.ds(g * GROUP, GROUP)
        return pltpu.make_async_remote_copy(
            src_ref=outbox.at[m, n, some],
            dst_ref=inbox.at[m, n, some],
            send_sem=part_sent.at[m, n, h],
            recv_sem=part_got.at[m, n, h],
            device_id=toward(m, h),
            device_id_type=MESH,
        )

    def half(ref, m, n, h):
        return ref.at[m, n, pl.ds(h * HELD, HELD)]

    def scale_copy(m, n, h):
        return pltpu.make_async_remote_copy(
            src_ref=half(outscale, m, n, h),
            dst_ref=half(inscale, m, n, h),
            send_sem=scale_sent.at[m, n, h],
            recv_sem=scale_got.at[m, n, h],
            device_id=toward(m, h),
            device_id_type=MESH,
        )

    def multiply(n, h):
        direct, held = (2, 0) if h == 0 else (0, 2)
        rows = 3 if n == 3 else 4

        def group(g, carry):
            def one(t, carry):
                p = g * GROUP + t
                i = jnp.clip(pairs[0, p] - start, 0, OCC_DEV - 1)
                j = jnp.clip(pairs[1, p] - start, 0, 2 * OCC_DEV - 1)
                block = jnp.dot(left[i, :rows * COL, :], cols[n][j], preferred_element_type=jnp.float32)
                for m in range(rows):
                    part = block[m * COL:(m + 1) * COL] * weight(p, m, n)
                    if m == 3:
                        total[n, p] = part
                    elif m == held:
                        hold[h, n, p - h * HELD] = part
                    else:
                        pack(p, m, n, part)
                return carry

            lax.fori_loop(0, GROUP, one, 0, unroll=UNROLL)
            part_copy(1, n, h, g).start()
            part_copy(direct, n, h, g).start()
            return carry

        lax.fori_loop(h * (HELD // GROUP), (h + 1) * (HELD // GROUP), group, 0)
        scale_copy(1, n, h).start()
        scale_copy(direct, n, h).start()

    def relay(n, h):
        m = 0 if h == 0 else 2
        wait_bytes(half(inbox, 1, n, h), part_got.at[1, n, h])
        wait_bytes(half(inscale, 1, n, h), scale_got.at[1, n, h])

        def group(g, carry):
            def one(t, carry):
                p = g * GROUP + t
                pack(p, m, n, hold[h, n, p - h * HELD] + unpack(p, 1, n))
                return carry

            lax.fori_loop(0, GROUP, one, 0, unroll=UNROLL)
            part_copy(m, n, h, g).start()
            return carry

        lax.fori_loop(h * (HELD // GROUP), (h + 1) * (HELD // GROUP), group, 0)
        scale_copy(m, n, h).start()

    def multiply_own(n):
        def one(p, carry):
            i = jnp.clip(pairs[0, p] - start, 0, OCC_DEV - 1)
            j = jnp.clip(pairs[1, p] - start, 0, 2 * OCC_DEV - 1)
            part = jnp.dot(left[i, 3 * COL:, :], cols[n][j], preferred_element_type=jnp.float32)
            total[n, p] = part * weight(p, 3, n)
            return carry

        lax.fori_loop(0, PAIRS_DEV, one, 0, unroll=UNROLL)

    def finish(n, h):
        for m in (0, 2):
            wait_bytes(half(inbox, m, n, h), part_got.at[m, n, h])
            wait_bytes(half(inscale, m, n, h), scale_got.at[m, n, h])

        def one(p, carry):
            out[p, :, column(n)] = (total[n, p] + unpack(p, 0, n) + unpack(p, 2, n)).astype(BF16)
            return carry

        lax.fori_loop(h * HELD, (h + 1) * HELD, one, 0)

    @pl.when(core == 0)
    def _():
        for q in range(4):
            arrived("A", q, N_OCC - 1)
            settle(q)

    @pl.when(core == 1)
    def _():
        for q in range(4):
            arrived("B", q, CHIPS - 1)
            middle_copy(q).start()
        for q in range(4):
            middle_copy(q).wait()
            settle(q)

    for n in range(4):
        @pl.when(core == 0)
        def _():
            arrived("B", n, CHIPS - 1)
            middle_copy(n).start()
            middle_copy(n).wait()

        @pl.when(core == 1)
        def _():
            arrived("C", n, N_OCC - 1)

        multiply(n, 0)
        if n > 0:
            relay(n - 1, 0)
            relay(n - 1, 1)
        multiply(n, 1)

    relay(3, 0)
    relay(3, 1)
    multiply_own(3)
    for n in range(4):
        for h in range(2):
            finish(n, h)

    for e, (part, q) in enumerate(EVENTS):
        wait_bytes(orbitals(q, CHIPS - 1), sent.at[e])
        if part != "B":
            @pl.when(core == (part == "A"))
            def _():
                wait_bytes(orbitals(q, 1), sent.at[e])

    for n in range(4):
        for m in range(3):
            for h in range(2):
                wait_bytes(half(outbox, m, n, h), part_sent.at[m, n, h])
                wait_bytes(half(outscale, m, n, h), scale_sent.at[m, n, h])


def on_device(slab, domain_class, pairs):
    dma = pltpu.SemaphoreType.DMA
    return pl.pallas_call(
        kernel,
        out_shape=jax.ShapeDtypeStruct((PAIRS_DEV, COL, DOM), BF16),
        in_specs=[
            pl.BlockSpec(memory_space=pltpu.SMEM),
            pl.BlockSpec(memory_space=pltpu.SMEM),
            pl.BlockSpec(memory_space=pl.ANY),
        ],
        out_specs=pl.BlockSpec(memory_space=pltpu.VMEM),
        scratch_shapes=[pltpu.VMEM((2 * OCC_DEV, KLOC, COL), BF16)] * 4 + [
            pltpu.VMEM((OCC_DEV, DOM, KLOC), BF16),
            pltpu.VMEM((4, PAIRS_DEV, COL, COL), jnp.float32),
            pltpu.VMEM((2, 4, HELD, COL, COL), jnp.float32),
            pltpu.VMEM((3, 4, PAIRS_DEV, COL, COL), jnp.int16),
            pltpu.VMEM((3, 4, PAIRS_DEV, COL, COL), jnp.int16),
            pltpu.VMEM((3, 4, PAIRS_DEV, COL), jnp.float32),
            pltpu.VMEM((3, 4, PAIRS_DEV, COL), jnp.float32),
            dma((12,)), dma((12,)), dma((12,)), dma((4,)), dma((4,)),
            dma((3, 4, 2)), dma((3, 4, 2)), dma((3, 4, 2)), dma((3, 4, 2)),
        ],
        compiler_params=pltpu.CompilerParams(
            collective_id=0, has_side_effects=True, vmem_limit_bytes=58 << 20
        ),
        cost_estimate=pl.CostEstimate(flops=17_000_000_000, bytes_accessed=12 << 20, transcendentals=0),
    )(domain_class, pairs.T, slab)


def solution(mesh):
    in_specs = (P(None, ("aux", "occ"), None), P(), P("occ", None))
    out_specs = P("occ", "aux", None)
    return jax.shard_map(
        on_device, mesh=mesh, in_specs=in_specs, out_specs=out_specs, check_vma=False
    )
```

```python
import functools

import jax
import jax.numpy as jnp
from jax import lax
from jax.experimental import pallas as pl
from jax.experimental.pallas import tpu as pltpu
from jax.sharding import PartitionSpec as P

DOM = 512
SLAB = 8192
OCC_DEV = 4
PAIRS_DEV = 16
N_AUX = 4
SIDE = 4
CHIPS = SIDE * SIDE
N_OCC = 2 * CHIPS
ROWS = 64
KLOC = N_OCC * ROWS
HALF = KLOC // 2
COL = DOM // 4
GROUP = 4
UNROLL = 4
NOCC = N_OCC * OCC_DEV
MESH = pl.DeviceIdType.MESH
LEVELS = 32767.0
TINY = 1e-33
BF16 = jnp.bfloat16
EVENTS = tuple((part, q) for part in "ABC" for q in range(4))
HELD = PAIRS_DEV // 2
FARTHEST = sorted(
    [(dz, dx) for dz in range(SIDE) for dx in range(SIDE) if dz or dx],
    key=lambda d: -sum(min(step, SIDE - step) for step in d),
)


def kernel(classes, pairs, slab, out, *scratch):
    cols = scratch[:4]
    (left, total, hold, outbox, inbox, outscale, inscale,
     got, sent, kept, mid_got, mid_sent, part_got, part_sent, scale_got, scale_sent) = scratch[4:]
    a = lax.axis_index("aux")
    o = lax.axis_index("occ")
    chip = o // 2
    core = lax.rem(o, 2)
    z, x = chip // SIDE, lax.rem(chip, SIDE)
    start = o * OCC_DEV
    sibling = o + 1 - 2 * core
    mine = pl.ds(core * HALF + chip * ROWS, ROWS)

    barrier = pltpu.get_barrier_semaphore()

    def greet_occ(s, carry):
        pl.semaphore_signal(barrier, inc=1, device_id=(a, lax.rem(o + s, N_OCC)), device_id_type=MESH)
        return carry

    def greet_aux(s, carry):
        pl.semaphore_signal(barrier, inc=1, device_id=(lax.rem(a + s, N_AUX), o), device_id_type=MESH)
        return carry

    lax.fori_loop(1, N_OCC, greet_occ, 0)
    greet_aux(1, 0)
    greet_aux(N_AUX - 1, 0)

    def column(q):
        return pl.ds(q * COL, COL)

    def place(part, to_chip):
        if part == "A":
            return 8 * to_chip, 0, 0
        if part == "B":
            return 8 * to_chip + 4, core, 4 - 4 * core
        return lax.rem(8 * to_chip + 8, NOCC), 1, 4

    def keep_copy(part, q):
        orbital, _, slot = place(part, chip)
        e = EVENTS.index((part, q))
        return pltpu.make_async_copy(
            slab.at[pl.ds(orbital, 4), :, column(q)], cols[q].at[pl.ds(slot, 4), mine, :], kept.at[e]
        )

    def slab_copy(part, q, to_chip):
        orbital, to_core, slot = place(part, to_chip)
        e = EVENTS.index((part, q))
        return pltpu.make_async_remote_copy(
            src_ref=slab.at[pl.ds(orbital, 4), :, column(q)],
            dst_ref=cols[q].at[pl.ds(slot, 4), mine, :],
            send_sem=sent.at[e],
            recv_sem=got.at[e],
            device_id=(a, 2 * to_chip + to_core),
            device_id_type=MESH,
        )

    for part, q in EVENTS:
        if part == "B":
            keep_copy(part, q).start()
        else:
            @pl.when(core == (part == "C"))
            def _():
                keep_copy(part, q).start()

    pl.semaphore_wait(barrier, N_OCC + 1)

    def send(part, q):
        if part != "B":
            @pl.when(core == (part == "A"))
            def _():
                slab_copy(part, q, chip).start()

        for dz, dx in FARTHEST:
            dz = dz + core * ((SIDE - dz) % SIDE - dz)
            dx = dx + core * ((SIDE - dx) % SIDE - dx)
            to = lax.rem(z + dz, SIDE) * SIDE + lax.rem(x + dx, SIDE)
            slab_copy(part, q, to).start()

    for part, q in EVENTS:
        send(part, q)

    def wait_bytes(ref, sem):
        pltpu.make_async_copy(ref, ref, sem).wait()

    def orbitals(q, sources):
        return cols[q].at[pl.ds(0, 4), pl.ds(0, sources * ROWS), :]

    def middle_copy(q):
        half = pl.ds(core * HALF, HALF)
        return pltpu.make_async_remote_copy(
            src_ref=cols[q].at[pl.ds(4 - 4 * core, 4), half, :],
            dst_ref=cols[q].at[pl.ds(4 * core, 4), half, :],
            send_sem=mid_sent.at[q],
            recv_sem=mid_got.at[q],
            device_id=(a, sibling),
            device_id_type=MESH,
        )

    def arrived(part, q, sources):
        e = EVENTS.index((part, q))
        wait_bytes(orbitals(q, 1), kept.at[e])
        wait_bytes(orbitals(q, sources), got.at[e])

    def settle(q):
        slot = pl.multiple_of(lax.rem(q + 7 - a, 4) * COL, COL)
        for i in range(OCC_DEV):
            left[i, pl.ds(slot, COL), :] = cols[q][i].T

    factor = 1.0 / jnp.sqrt(jnp.float32(SLAB))

    def weight(p, m, n):
        keep_m = lax.rem(a + m + 1, 4) <= classes[pairs[0, p]]
        keep_n = n <= classes[pairs[1, p]]
        return jnp.where(jnp.logical_and(keep_m, keep_n), factor, 0.0)

    def pack(p, m, n, block):
        top = jnp.maximum(jnp.max(jnp.abs(block), axis=0, keepdims=True), TINY)
        outscale[m, n, pl.ds(p, 1), :] = top * (1.0 / LEVELS)
        outbox[m, n, p] = jnp.round(block * (LEVELS / top)).astype(jnp.int32).astype(jnp.int16)

    def unpack(p, m, n):
        return inbox[m, n, p].astype(jnp.int32).astype(jnp.float32) * inscale[m, n, pl.ds(p, 1), :]

    def toward(m, h):
        up = m == 0 or (m == 1 and h == 0)
        return lax.rem(a + (1 if up else N_AUX - 1), N_AUX), o

    def part_copy(m, n, h, g):
        some = pl.ds(g * GROUP, GROUP)
        return pltpu.make_async_remote_copy(
            src_ref=outbox.at[m, n, some],
            dst_ref=inbox.at[m, n, some],
            send_sem=part_sent.at[m, n, h],
            recv_sem=part_got.at[m, n, h],
            device_id=toward(m, h),
            device_id_type=MESH,
        )

    def half(ref, m, n, h):
        return ref.at[m, n, pl.ds(h * HELD, HELD)]

    def scale_copy(m, n, h):
        return pltpu.make_async_remote_copy(
            src_ref=half(outscale, m, n, h),
            dst_ref=half(inscale, m, n, h),
            send_sem=scale_sent.at[m, n, h],
            recv_sem=scale_got.at[m, n, h],
            device_id=toward(m, h),
            device_id_type=MESH,
        )

    def multiply(n, h):
        direct, held = (2, 0) if h == 0 else (0, 2)
        rows = 3 if n == 3 else 4

        def group(g, carry):
            def one(t, carry):
                p = g * GROUP + t
                i = jnp.clip(pairs[0, p] - start, 0, OCC_DEV - 1)
                j = jnp.clip(pairs[1, p] - start, 0, 2 * OCC_DEV - 1)
                block = jnp.dot(left[i, :rows * COL, :], cols[n][j], preferred_element_type=jnp.float32)
                for m in range(rows):
                    part = block[m * COL:(m + 1) * COL] * weight(p, m, n)
                    if m == 3:
                        total[n, p] = part
                    elif m == held:
                        hold[h, n, p - h * HELD] = part
                    else:
                        pack(p, m, n, part)
                return carry

            lax.fori_loop(0, GROUP, one, 0, unroll=UNROLL)
            part_copy(1, n, h, g).start()
            part_copy(direct, n, h, g).start()
            return carry

        lax.fori_loop(h * (HELD // GROUP), (h + 1) * (HELD // GROUP), group, 0)
        scale_copy(1, n, h).start()
        scale_copy(direct, n, h).start()

    def relay(n, h):
        m = 0 if h == 0 else 2
        wait_bytes(half(inbox, 1, n, h), part_got.at[1, n, h])
        wait_bytes(half(inscale, 1, n, h), scale_got.at[1, n, h])

        def group(g, carry):
            def one(t, carry):
                p = g * GROUP + t
                pack(p, m, n, hold[h, n, p - h * HELD] + unpack(p, 1, n))
                return carry

            lax.fori_loop(0, GROUP, one, 0, unroll=UNROLL)
            part_copy(m, n, h, g).start()
            return carry

        lax.fori_loop(h * (HELD // GROUP), (h + 1) * (HELD // GROUP), group, 0)
        scale_copy(m, n, h).start()

    def multiply_own(n):
        def one(p, carry):
            i = jnp.clip(pairs[0, p] - start, 0, OCC_DEV - 1)
            j = jnp.clip(pairs[1, p] - start, 0, 2 * OCC_DEV - 1)
            part = jnp.dot(left[i, 3 * COL:, :], cols[n][j], preferred_element_type=jnp.float32)
            total[n, p] = part * weight(p, 3, n)
            return carry

        lax.fori_loop(0, PAIRS_DEV, one, 0, unroll=UNROLL)

    def finish(n, h):
        for m in (0, 2):
            wait_bytes(half(inbox, m, n, h), part_got.at[m, n, h])
            wait_bytes(half(inscale, m, n, h), scale_got.at[m, n, h])

        def one(p, carry):
            out[p, :, column(n)] = (total[n, p] + unpack(p, 0, n) + unpack(p, 2, n)).astype(BF16)
            return carry

        lax.fori_loop(h * HELD, (h + 1) * HELD, one, 0)

    @pl.when(core == 0)
    def _():
        for q in range(4):
            arrived("A", q, N_OCC - 1)
            settle(q)

    @pl.when(core == 1)
    def _():
        for q in range(4):
            arrived("B", q, CHIPS - 1)
            middle_copy(q).start()
        for q in range(4):
            middle_copy(q).wait()
            settle(q)

    for n in range(4):
        @pl.when(core == 0)
        def _():
            arrived("B", n, CHIPS - 1)
            middle_copy(n).start()
            middle_copy(n).wait()

        @pl.when(core == 1)
        def _():
            arrived("C", n, N_OCC - 1)

        multiply(n, 0)
        if n > 0:
            relay(n - 1, 0)
            relay(n - 1, 1)
        multiply(n, 1)

    relay(3, 0)
    relay(3, 1)
    multiply_own(3)
    for n in range(4):
        for h in range(2):
            finish(n, h)

    for e, (part, q) in enumerate(EVENTS):
        wait_bytes(orbitals(q, CHIPS - 1), sent.at[e])
        if part != "B":
            @pl.when(core == (part == "A"))
            def _():
                wait_bytes(orbitals(q, 1), sent.at[e])

    for n in range(4):
        for m in range(3):
            for h in range(2):
                wait_bytes(half(outbox, m, n, h), part_sent.at[m, n, h])
                wait_bytes(half(outscale, m, n, h), scale_sent.at[m, n, h])


def store(sums, out):
    out[...] = sums[...]


def on_device(slab, domain_class, pairs):
    dma = pltpu.SemaphoreType.DMA
    sums = pl.pallas_call(
        kernel,
        out_shape=jax.ShapeDtypeStruct((PAIRS_DEV, COL, DOM), BF16),
        in_specs=[
            pl.BlockSpec(memory_space=pltpu.SMEM),
            pl.BlockSpec(memory_space=pltpu.SMEM),
            pl.BlockSpec(memory_space=pl.ANY),
        ],
        out_specs=pl.BlockSpec(memory_space=pltpu.VMEM),
        scratch_shapes=[pltpu.VMEM((2 * OCC_DEV, KLOC, COL), BF16)] * 4 + [
            pltpu.VMEM((OCC_DEV, DOM, KLOC), BF16),
            pltpu.VMEM((4, PAIRS_DEV, COL, COL), jnp.float32),
            pltpu.VMEM((2, 4, HELD, COL, COL), jnp.float32),
            pltpu.VMEM((3, 4, PAIRS_DEV, COL, COL), jnp.int16),
            pltpu.VMEM((3, 4, PAIRS_DEV, COL, COL), jnp.int16),
            pltpu.VMEM((3, 4, PAIRS_DEV, COL), jnp.float32),
            pltpu.VMEM((3, 4, PAIRS_DEV, COL), jnp.float32),
            dma((12,)), dma((12,)), dma((12,)), dma((4,)), dma((4,)),
            dma((3, 4, 2)), dma((3, 4, 2)), dma((3, 4, 2)), dma((3, 4, 2)),
        ],
        compiler_params=pltpu.CompilerParams(
            collective_id=0, has_side_effects=True, vmem_limit_bytes=58 << 20
        ),
        cost_estimate=pl.CostEstimate(flops=17_000_000_000, bytes_accessed=12 << 20, transcendentals=0),
    )(domain_class, pairs.T, slab)
    block = pl.BlockSpec((PAIRS_DEV // 4, COL, DOM), lambda s: (s, 0, 0))
    return pl.pallas_call(
        store,
        grid=(4,),
        out_shape=jax.ShapeDtypeStruct((PAIRS_DEV, COL, DOM), BF16),
        in_specs=[block],
        out_specs=block,
    )(sums)


def solution(mesh):
    in_specs = (P(None, ("aux", "occ"), None), P(), P("occ", None))
    out_specs = P("occ", "aux", None)
    return jax.shard_map(
        on_device, mesh=mesh, in_specs=in_specs, out_specs=out_specs, check_vma=False
    )
```
